32 devices in a mesh: curves: 8 (over z, x), tm: 4 (over y, core).
Axes of the slice: x: 2, y: 2, z: 4, core: 2. Of those that a mesh axis runs over, the one named last changes fastest.
Arguments:
- curves_data: float32 [6144, 16384], P('curves', 'tm'), as said below
- loadings: float32 [6144, 256], P('curves'), may hold values from 0 to 10, as said below
- profiles: float32 [16384, 256], P('tm'), may hold values from 0 to 5, as said below
- counts: int32 [8], replicated, may hold values from 1 to 768, as said below
Outputs:
- new_loadings: float32 [6144, 256], P('curves')
- new_profiles: float32 [16384, 256], P('tm')
The draws below stay inside these ranges and needn't reach their ends.
Inputs may be any that keep to these rules, and one draw needn't show every extreme that they name: counts[i] curves of campaign i fill the first slots of its 768; for i < 4, the blocks of 128 slots that campaigns i and i + 4 occupy (each rounded up) total at most 8; some campaign fills all its slots. `loadings`: nonnegative. `profiles`: nonnegative. `curves_data`: nonnegative.
All inputs are finite; a program needn't handle non-finite values.
Results may differ from the reference program's by a relative error of at most 0.00025.
Values sent between devices are 32-bit elements; how exact they have to be, the bound alone decides.
A program may use at most 128 MiB of HBM per device.

```python
import math
import jax
import jax.numpy as jnp
from jax import lax

COMPS = 256
TPTS = 16384
BLOCK = 128
MAXBLK = 6
PAIRBLK = 4
ROWS = 768
CURVES_ALL = 6144
N_CURVES = 8


def make_loadings(key):
    first, second = jax.random.split(jax.random.fold_in(key, 11), 2)
    base = jnp.exp(jax.random.uniform(first, (CURVES_ALL, COMPS), jnp.float32, math.log(0.05), math.log(0.5)))
    column = jnp.exp(jax.random.uniform(second, (1, COMPS), jnp.float32, math.log(0.5), math.log(2.0)))
    where_at = jnp.arange(CURVES_ALL, dtype=jnp.float32) / CURVES_ALL
    rising = 1.0 + 2.0 * where_at
    return (base * column * rising[:, None]).astype(jnp.float32)


def make_profiles(key):
    first, second, third = jax.random.split(jax.random.fold_in(key, 12), 3)
    base = jnp.exp(jax.random.uniform(first, (TPTS, COMPS), jnp.float32, math.log(0.05), math.log(0.5)))
    column = jnp.exp(jax.random.uniform(second, (1, COMPS), jnp.float32, math.log(0.3), math.log(3.0)))
    scale_rows = jnp.exp(jax.random.uniform(third, (TPTS,), jnp.float32, math.log(0.3), math.log(3.0)))
    return (base * column * scale_rows[:, None]).astype(jnp.float32)


def draw_loadings(key, part):
    return make_loadings(key)


def draw_profiles(key, part):
    return make_profiles(key)


def draw_curves_data(key, part):
    fitted = jnp.dot(make_loadings(key), make_profiles(key).T, precision=lax.Precision.HIGHEST)
    noise_key = jax.random.fold_in(key, 13)
    noise = 0.4 * jax.random.uniform(noise_key, (CURVES_ALL, TPTS), jnp.float32, -1.0, 1.0)
    return (fitted * (1.0 + noise)).astype(jnp.float32)


def draw_counts(key, part):
    half = N_CURVES // 2
    key_heavy, key_light, key_side, key_pick = jax.random.split(jax.random.fold_in(key, 14), 4)
    heavy = jax.random.randint(key_heavy, (half,), 1, ROWS + 1)
    forced = jax.random.randint(key_pick, (), 0, half)
    heavy = jnp.where(jnp.arange(half) == forced, ROWS, heavy)
    heavy_blocks = (heavy + BLOCK - 1) // BLOCK
    room = jnp.minimum(2 * PAIRBLK - heavy_blocks, MAXBLK) * BLOCK
    light = jax.random.randint(key_light, (half,), 1, room + 1)
    side = jax.random.randint(key_side, (half,), 0, 2)
    first = jnp.where(side == 1, heavy, light)
    second = jnp.where(side == 1, light, heavy)
    return jnp.concatenate([first, second]).astype(jnp.int32)


def setup_inputs(seed: int = 0) -> dict:
    arg_keys = jax.random.split(jax.random.key(seed), 5)
    curves_data = draw_curves_data(jax.random.fold_in(arg_keys[4], 71), 0)
    loadings = draw_loadings(jax.random.fold_in(arg_keys[4], 71), 0)
    profiles = draw_profiles(jax.random.fold_in(arg_keys[4], 71), 0)
    counts = draw_counts(jax.random.fold_in(arg_keys[4], 71), 0)
    return dict(curves_data=curves_data, loadings=loadings, profiles=profiles, counts=counts)


def reference(curves_data, loadings, profiles, counts):
    high = lax.Precision.HIGHEST
    data = curves_data.reshape(N_CURVES, ROWS, TPTS)
    load = loadings.reshape(N_CURVES, ROWS, COMPS)
    live = lax.iota(jnp.int32, ROWS)[None, :] < counts[:, None]

    def campaign(total, item):
        block, weights, alive = item
        recon = jnp.dot(weights, profiles.T, precision=high)
        resid = jnp.where(alive[:, None], block - recon, 0.0)
        row_grad = jnp.dot(resid, profiles, precision=high)
        total = total + jnp.dot(resid.T, weights, precision=high)
        return total, row_grad

    time_grad, row_grad = lax.scan(campaign, jnp.zeros((TPTS, COMPS), jnp.float32), (data, load, live))
    row_grad = row_grad.reshape(N_CURVES * ROWS, COMPS)
    alive = live.reshape(N_CURVES * ROWS)[:, None]
    time_norm = jnp.sum(profiles * profiles, axis=0)
    curve_norm = jnp.sum(jnp.where(alive, loadings * loadings, 0.0), axis=0)
    new_loadings = jnp.where(alive, jnp.maximum(loadings + row_grad / time_norm, 0.0), 0.0)
    new_profiles = jnp.maximum(profiles + time_grad / curve_norm, 0.0)
    return new_loadings, new_profiles
```

```python
import functools

import jax
import jax.numpy as jnp
from jax import lax
from jax.experimental import pallas as pl
from jax.experimental.pallas import tpu as pltpu
from jax.sharding import PartitionSpec as P

MESH = pl.DeviceIdType.MESH
NORM_ROWS = 8


def split(value):
    high = value.astype(jnp.bfloat16)
    low = (value - high.astype(jnp.float32)).astype(jnp.bfloat16)
    return high, low


def dot3(a, b, contract):
    dims = (contract, ((), ()))
    mul = lambda x, y: lax.dot_general(x, y, dims, preferred_element_type=jnp.float32)
    return mul(a[0], b[0]) + (mul(a[0], b[1]) + mul(a[1], b[0]))


def kernel(
    n, ntm, pieces, sub,
    counts_ref, data_ref, load_ref, prof_ref,
    new_load_ref, new_prof_ref,
    data_v, prof_v, load_h, load_l, loadt_h, loadt_l,
    grad, came, full, norms, rows_out, rows_in, rows_new,
    data_sem, prof_sem, ring_send, ring_recv, all_send, all_recv, norm_send, norm_recv,
    row_send, row_recv, new_send, new_recv, out_sem, rows_sem,
):
    slots, comps = load_ref.shape
    chunk = prof_v.shape[1]
    half = comps // 2
    part = chunk // pieces
    span = slots // ntm
    curve = lax.axis_index("curves")
    shard = lax.axis_index("tm")

    line = curve // 2
    me = jnp.where(curve % 2 == 0, line, n - 1 - line)

    def device_at(place):
        place = lax.rem(place + n, n)
        return jnp.where(place < n // 2, 2 * place, 2 * (n - 1 - place) + 1)

    ways = ((1, device_at(me + 1)), (-1, device_at(me - 1)))
    peers = [lax.rem(shard + k, ntm) for k in range(1, ntm)]

    barrier = pltpu.get_barrier_semaphore()
    for _, other in ways:
        pl.semaphore_signal(barrier, inc=1, device_id={"curves": other}, device_id_type=MESH)
    for other in peers:
        pl.semaphore_signal(barrier, inc=1, device_id={"tm": other}, device_id_type=MESH)

    def chunk_at(order):
        step = (order + 1) // 2
        return lax.rem(jnp.where(order % 2 == 1, me - step, me + step) + n, n)

    def loads(order):
        c = chunk_at(order)
        start = pl.multiple_of(c * chunk, chunk)
        return (
            pltpu.make_async_copy(data_ref.at[:, pl.ds(start, chunk)], data_v.at[c], data_sem.at[c]),
            pltpu.make_async_copy(prof_ref.at[pl.ds(start, chunk), :], prof_v.at[c], prof_sem.at[c]),
        )

    def start_loads(order, carry):
        for copy in loads(order):
            copy.start()
        return carry

    lax.fori_loop(0, n, start_loads, 0)

    own = counts_ref[curve]
    keep = lax.broadcasted_iota(jnp.int32, (slots, 1), 0) < own
    load = load_ref[...]
    load_h[...], load_l[...] = split(load)
    loadt_h[...], loadt_l[...] = split(load.T)
    norm = jnp.sum(jnp.where(keep, load * load, 0.0), axis=0, keepdims=True)
    norms[me] = jnp.broadcast_to(norm, (NORM_ROWS, comps))
    rows_out[...] = jnp.zeros_like(rows_out)

    def compute(order, carry):
        c = chunk_at(order)
        for copy in loads(order):
            copy.wait()

        def piece(u, inner):
            start = pl.multiple_of(u * sub, sub)
            prof = prof_v[c, pl.ds(start, sub), :]
            prof2 = split(prof)
            load2 = (load_h[...], load_l[...])
            recon = dot3(load2, prof2, ((1,), (1,)))
            resid = jnp.where(keep, data_v[c, :, pl.ds(start, sub)] - recon, 0.0)
            resid2 = split(resid)
            row = dot3(resid2, prof2, ((1,), (0,)))
            square = jnp.broadcast_to(jnp.sum(prof * prof, axis=0, keepdims=True), (NORM_ROWS, comps))
            for o in range(ntm):
                rows_out[o, :span, :] += row[o * span:(o + 1) * span]
                rows_out[o, span:, :] += square
            time = dot3((loadt_h[...], loadt_l[...]), resid2, ((1,), (0,))).T
            grad[0, c, pl.ds(start, sub), :] = time[:, :half]
            grad[1, c, pl.ds(start, sub), :] = time[:, half:]
            return inner

        lax.fori_loop(0, chunk // sub, piece, 0)
        return carry

    def row_copy(k):
        other = peers[k]
        return pltpu.make_async_remote_copy(
            src_ref=rows_out.at[other], dst_ref=rows_in.at[k],
            send_sem=row_send.at[k], recv_sem=row_recv.at[k],
            device_id={"tm": other}, device_id_type=MESH,
        )

    def new_copy(k):
        return pltpu.make_async_remote_copy(
            src_ref=rows_new.at[shard], dst_ref=rows_new.at[shard],
            send_sem=new_send.at[k], recv_sem=new_recv.at[k],
            device_id={"tm": peers[k]}, device_id_type=MESH,
        )

    def ring_copy(w, step, piece):
        sign, other = ways[w]
        c = lax.rem(me - sign * step + 2 * n, n)
        at = pl.ds(piece * part, part)
        return c, at, pltpu.make_async_remote_copy(
            src_ref=grad.at[w, c, at, :], dst_ref=came.at[w, step, at, :],
            send_sem=ring_send.at[w, step, piece], recv_sem=ring_recv.at[w, step, piece],
            device_id={"curves": other}, device_id_type=MESH,
        )

    def norm_copy(step):
        c = lax.rem(me - step + 2 * n, n)
        return pltpu.make_async_remote_copy(
            src_ref=norms.at[c], dst_ref=norms.at[c],
            send_sem=norm_send.at[step], recv_sem=norm_recv.at[step],
            device_id={"curves": ways[0][1]}, device_id_type=MESH,
        )

    def all_copy(w, step, piece):
        sign, other = ways[w]
        c = lax.rem(me + sign - sign * step + 2 * n, n)
        at = pl.ds(piece * part, part)
        return pltpu.make_async_remote_copy(
            src_ref=full.at[w, c, at, :], dst_ref=full.at[w, c, at, :],
            send_sem=all_send.at[w, step, piece], recv_sem=all_recv.at[w, step, piece],
            device_id={"curves": other}, device_id_type=MESH,
        )

    def out_copy(w, step, piece):
        sign, _ = ways[w]
        c = lax.rem(me + sign - sign * step + 2 * n, n)
        rows = pl.ds(pl.multiple_of(c * chunk + piece * part, part), part)
        return pltpu.make_async_copy(
            full.at[w, c, pl.ds(piece * part, part), :],
            new_prof_ref.at[rows, pl.ds(w * half, half)],
            out_sem.at[w, step, piece],
        )

    pl.semaphore_wait(barrier, 2 + len(peers))

    def ring_step(step, carry):
        lax.fori_loop(jnp.maximum(2 * step - 1, 0), jnp.minimum(2 * step + 1, n), compute, 0)

        @pl.when(step == n // 2)
        def _():
            for k in range(ntm - 1):
                row_copy(k).start()

        for piece in range(pieces):
            for w in range(2):
                c, at, copy = ring_copy(w, step, piece)

                @pl.when(step > 0)
                def _():
                    ring_copy(w, step - 1, piece)[2].wait_recv()
                    grad[w, c, at, :] = grad[w, c, at, :] + came[w, step - 1, at, :]

                copy.start()

        @pl.when(step > 0)
        def _():
            norm_copy(step - 1).wait_recv()

        norm_copy(step).start()
        return carry

    lax.fori_loop(0, n - 1, ring_step, 0)

    norm_copy(n - 2).wait_recv()
    total = norms[0]
    for k in range(1, n):
        total = total + norms[k]
    total = total[0:1]

    for piece in range(pieces):
        for w in range(2):
            ring_copy(w, n - 2, piece)[2].wait_recv()
            sign, _ = ways[w]
            c = lax.rem(me + sign + n, n)
            at = pl.ds(piece * part, part)
            lanes = pl.ds(w * half, half)
            summed = grad[w, c, at, :] + came[w, n - 2, at, :]
            full[w, c, at, :] = jnp.maximum(
                prof_v[c, at, lanes] + summed / total[:, w * half:(w + 1) * half], 0.0
            )
            all_copy(w, 0, piece).start()
            out_copy(w, 0, piece).start()

    for k in range(ntm - 1):
        row_copy(k).wait()
    mine = rows_out[shard]
    for k in range(ntm - 1):
        mine = mine + rows_in[k]
    base = pl.multiple_of(shard * span, span)
    alive = base + lax.broadcasted_iota(jnp.int32, (span, 1), 0) < own
    moved = load_ref[pl.ds(base, span), :] + mine[:span] / mine[span:span + 1]
    rows_new[shard] = jnp.where(alive, jnp.maximum(moved, 0.0), 0.0)
    for k in range(ntm - 1):
        new_copy(k).start()

    def all_step(step, carry):
        for piece in range(pieces):
            for w in range(2):
                all_copy(w, step - 1, piece).wait_recv()
                all_copy(w, step, piece).start()
                out_copy(w, step, piece).start()
        return carry

    lax.fori_loop(1, n - 1, all_step, 0)

    for k in range(ntm - 1):
        new_copy(k).wait()
    for o in range(ntm):
        pltpu.make_async_copy(
            rows_new.at[o], new_load_ref.at[pl.ds(o * span, span), :], rows_sem.at[o]
        ).start()

    for piece in range(pieces):
        for w in range(2):
            all_copy(w, n - 2, piece).wait_recv()
            out_copy(w, n - 1, piece).start()

    def drain(step, carry):
        for piece in range(pieces):
            for w in range(2):
                ring_copy(w, step, piece)[2].wait_send()
                all_copy(w, step, piece).wait_send()
                out_copy(w, step, piece).wait()
        norm_copy(step).wait_send()
        return carry

    lax.fori_loop(0, n - 1, drain, 0)
    for piece in range(pieces):
        for w in range(2):
            out_copy(w, n - 1, piece).wait()
    for o in range(ntm):
        pltpu.make_async_copy(
            rows_new.at[o], new_load_ref.at[pl.ds(o * span, span), :], rows_sem.at[o]
        ).wait()


def local(n, ntm, curves_data, loadings, profiles, counts):
    slots, points = curves_data.shape
    comps = loadings.shape[1]
    chunk = points // n
    sub = min(chunk, 256)
    pieces = 2
    half = comps // 2
    span = slots // ntm
    f32, bf16 = jnp.float32, jnp.bfloat16
    dma = pltpu.SemaphoreType.DMA
    flops = 3 * 3 * 2 * slots * points * comps
    return pl.pallas_call(
        functools.partial(kernel, n, ntm, pieces, sub),
        out_shape=(
            jax.ShapeDtypeStruct((slots, comps), f32),
            jax.ShapeDtypeStruct((points, comps), f32),
        ),
        in_specs=[
            pl.BlockSpec(memory_space=pltpu.SMEM),
            pl.BlockSpec(memory_space=pl.ANY),
            pl.BlockSpec(memory_space=pltpu.VMEM),
            pl.BlockSpec(memory_space=pl.ANY),
        ],
        out_specs=[pl.BlockSpec(memory_space=pl.ANY)] * 2,
        scratch_shapes=[
            pltpu.VMEM((n, slots, chunk), f32),
            pltpu.VMEM((n, chunk, comps), f32),
            pltpu.VMEM((slots, comps), bf16),
            pltpu.VMEM((slots, comps), bf16),
            pltpu.VMEM((comps, slots), bf16),
            pltpu.VMEM((comps, slots), bf16),
            pltpu.VMEM((2, n, chunk, half), f32),
            pltpu.VMEM((2, n - 1, chunk, half), f32),
            pltpu.VMEM((2, n, chunk, half), f32),
            pltpu.VMEM((n, NORM_ROWS, comps), f32),
            pltpu.VMEM((ntm, span + NORM_ROWS, comps), f32),
            pltpu.VMEM((ntm - 1, span + NORM_ROWS, comps), f32),
            pltpu.VMEM((ntm, span, comps), f32),
            dma((n,)),
            dma((n,)),
            dma((2, n - 1, pieces)),
            dma((2, n - 1, pieces)),
            dma((2, n - 1, pieces)),
            dma((2, n - 1, pieces)),
            dma((n - 1,)),
            dma((n - 1,)),
            dma((ntm - 1,)),
            dma((ntm - 1,)),
            dma((ntm - 1,)),
            dma((ntm - 1,)),
            dma((2, n, pieces)),
            dma((ntm,)),
        ],
        compiler_params=pltpu.CompilerParams(
            collective_id=0, has_side_effects=True, vmem_limit_bytes=56 * 1024 * 1024
        ),
        cost_estimate=pl.CostEstimate(
            flops=flops, bytes_accessed=4 * (slots * points + 2 * points * comps), transcendentals=0
        ),
    )(counts, curves_data, loadings, profiles)


def solution(mesh):
    return jax.shard_map(
        functools.partial(local, mesh.shape["curves"], mesh.shape["tm"]),
        mesh=mesh,
        in_specs=(P("curves", "tm"), P("curves", None), P("tm", None), P()),
        out_specs=(P("curves", None), P("tm", None)),
        check_vma=False,
    )
```

```python
import functools

import jax
import jax.numpy as jnp
from jax import lax
from jax.experimental import pallas as pl
from jax.experimental.pallas import tpu as pltpu
from jax.sharding import PartitionSpec as P

MESH = pl.DeviceIdType.MESH
NORM_ROWS = 8


def split(value):
    high = value.astype(jnp.bfloat16)
    low = (value - high.astype(jnp.float32)).astype(jnp.bfloat16)
    return high, low


def dot3(a, b, contract):
    dims = (contract, ((), ()))
    mul = lambda x, y: lax.dot_general(x, y, dims, preferred_element_type=jnp.float32)
    return mul(a[0], b[0]) + (mul(a[0], b[1]) + mul(a[1], b[0]))


def kernel(
    n, ntm, pieces, sub,
    counts_ref, data_ref, load_ref, prof_ref,
    new_load_ref, new_prof_ref,
    data_v, prof_v, load_h, load_l, loadt_h, loadt_l,
    grad, came, full, norms, rows_out, rows_in, rows_new,
    data_sem, prof_sem, ring_send, ring_recv, all_send, all_recv, norm_send, norm_recv,
    row_send, row_recv, new_send, new_recv, out_sem, rows_sem,
):
    slots, comps = load_ref.shape
    chunk = prof_v.shape[1]
    half = comps // 2
    part = chunk // pieces
    span = slots // ntm
    curve = lax.axis_index("curves")
    shard = lax.axis_index("tm")

    line = curve // 2
    me = jnp.where(curve % 2 == 0, line, n - 1 - line)

    def device_at(place):
        place = lax.rem(place + n, n)
        return jnp.where(place < n // 2, 2 * place, 2 * (n - 1 - place) + 1)

    ways = ((1, device_at(me + 1)), (-1, device_at(me - 1)))
    peers = [lax.rem(shard + k, ntm) for k in range(1, ntm)]

    barrier = pltpu.get_barrier_semaphore()
    for _, other in ways:
        pl.semaphore_signal(barrier, inc=1, device_id={"curves": other}, device_id_type=MESH)
    for other in peers:
        pl.semaphore_signal(barrier, inc=1, device_id={"tm": other}, device_id_type=MESH)

    def chunk_at(order):
        step = (order + 1) // 2
        return lax.rem(jnp.where(order % 2 == 1, me - step, me + step) + n, n)

    def loads(order):
        c = chunk_at(order)
        start = pl.multiple_of(c * chunk, chunk)
        return (
            pltpu.make_async_copy(data_ref.at[:, pl.ds(start, chunk)], data_v.at[c], data_sem.at[c]),
            pltpu.make_async_copy(prof_ref.at[pl.ds(start, chunk), :], prof_v.at[c], prof_sem.at[c]),
        )

    def start_loads(order, carry):
        for copy in loads(order):
            copy.start()
        return carry

    lax.fori_loop(0, n, start_loads, 0)

    own = counts_ref[curve]
    keep = lax.broadcasted_iota(jnp.int32, (slots, 1), 0) < own
    load = load_ref[...]
    load_h[...], load_l[...] = split(load)
    loadt_h[...], loadt_l[...] = split(load.T)
    norm = jnp.sum(jnp.where(keep, load * load, 0.0), axis=0, keepdims=True)
    norms[me] = jnp.broadcast_to(norm, (NORM_ROWS, comps))
    rows_out[...] = jnp.zeros_like(rows_out)

    def compute(order, carry):
        c = chunk_at(order)
        for copy in loads(order):
            copy.wait()

        def piece(u, inner):
            start = pl.multiple_of(u * sub, sub)
            prof = prof_v[c, pl.ds(start, sub), :]
            prof2 = split(prof)
            load2 = (load_h[...], load_l[...])
            recon = dot3(load2, prof2, ((1,), (1,)))
            resid = jnp.where(keep, data_v[c, :, pl.ds(start, sub)] - recon, 0.0)
            resid2 = split(resid)
            row = dot3(resid2, prof2, ((1,), (0,)))
            square = jnp.broadcast_to(jnp.sum(prof * prof, axis=0, keepdims=True), (NORM_ROWS, comps))
            for o in range(ntm):
                rows_out[o, :span, :] += row[o * span:(o + 1) * span]
                rows_out[o, span:, :] += square
            time = dot3((loadt_h[...], loadt_l[...]), resid2, ((1,), (0,))).T
            grad[0, c, pl.ds(start, sub), :] = time[:, :half]
            grad[1, c, pl.ds(start, sub), :] = time[:, half:]
            return inner

        lax.fori_loop(0, chunk // sub, piece, 0)
        return carry

    def row_copy(k):
        other = peers[k]
        return pltpu.make_async_remote_copy(
            src_ref=rows_out.at[other], dst_ref=rows_in.at[k],
            send_sem=row_send.at[k], recv_sem=row_recv.at[k],
            device_id={"tm": other}, device_id_type=MESH,
        )

    def new_copy(k):
        return pltpu.make_async_remote_copy(
            src_ref=rows_new.at[shard], dst_ref=rows_new.at[shard],
            send_sem=new_send.at[k], recv_sem=new_recv.at[k],
            device_id={"tm": peers[k]}, device_id_type=MESH,
        )

    def ring_copy(w, step, piece):
        sign, other = ways[w]
        c = lax.rem(me - sign * step + 2 * n, n)
        at = pl.ds(piece * part, part)
        return c, at, pltpu.make_async_remote_copy(
            src_ref=grad.at[w, c, at, :], dst_ref=came.at[w, step, at, :],
            send_sem=ring_send.at[w, step, piece], recv_sem=ring_recv.at[w, step, piece],
            device_id={"curves": other}, device_id_type=MESH,
        )

    def norm_copy(step):
        c = lax.rem(me - step + 2 * n, n)
        return pltpu.make_async_remote_copy(
            src_ref=norms.at[c], dst_ref=norms.at[c],
            send_sem=norm_send.at[step], recv_sem=norm_recv.at[step],
            device_id={"curves": ways[0][1]}, device_id_type=MESH,
        )

    def all_copy(w, step, piece):
        sign, other = ways[w]
        c = lax.rem(me + sign - sign * step + 2 * n, n)
        at = pl.ds(piece * part, part)
        return pltpu.make_async_remote_copy(
            src_ref=full.at[w, c, at, :], dst_ref=full.at[w, c, at, :],
            send_sem=all_send.at[w, step, piece], recv_sem=all_recv.at[w, step, piece],
            device_id={"curves": other}, device_id_type=MESH,
        )

    def out_copy(w, step, piece):
        sign, _ = ways[w]
        c = lax.rem(me + sign - sign * step + 2 * n, n)
        rows = pl.ds(pl.multiple_of(c * chunk + piece * part, part), part)
        return pltpu.make_async_copy(
            full.at[w, c, pl.ds(piece * part, part), :],
            new_prof_ref.at[rows, pl.ds(w * half, half)],
            out_sem.at[w, step, piece],
        )

    pl.semaphore_wait(barrier, 2 + len(peers))

    def ring_step(step, carry):
        lax.fori_loop(jnp.maximum(2 * step - 1, 0), jnp.minimum(2 * step + 1, n), compute, 0)

        @pl.when(step == n // 2)
        def _():
            for k in range(ntm - 1):
                row_copy(k).start()

        for piece in range(pieces):
            for w in range(2):
                c, at, copy = ring_copy(w, step, piece)

                @pl.when(step > 0)
                def _():
                    ring_copy(w, step - 1, piece)[2].wait_recv()
                    grad[w, c, at, :] = grad[w, c, at, :] + came[w, step - 1, at, :]

                copy.start()

        @pl.when(step > 0)
        def _():
            norm_copy(step - 1).wait_recv()

        norm_copy(step).start()
        return carry

    lax.fori_loop(0, n - 1, ring_step, 0)

    norm_copy(n - 2).wait_recv()
    total = norms[0]
    for k in range(1, n):
        total = total + norms[k]
    total = total[0:1]

    for piece in range(pieces):
        for w in range(2):
            ring_copy(w, n - 2, piece)[2].wait_recv()
            sign, _ = ways[w]
            c = lax.rem(me + sign + n, n)
            at = pl.ds(piece * part, part)
            lanes = pl.ds(w * half, half)
            summed = grad[w, c, at, :] + came[w, n - 2, at, :]
            full[w, c, at, :] = jnp.maximum(
                prof_v[c, at, lanes] + summed / total[:, w * half:(w + 1) * half], 0.0
            )
            all_copy(w, 0, piece).start()
            out_copy(w, 0, piece).start()

    for k in range(ntm - 1):
        row_copy(k).wait()
    mine = rows_out[shard]
    for k in range(ntm - 1):
        mine = mine + rows_in[k]
    base = pl.multiple_of(shard * span, span)
    alive = base + lax.broadcasted_iota(jnp.int32, (span, 1), 0) < own
    moved = load_ref[pl.ds(base, span), :] + mine[:span] / mine[span:span + 1]
    rows_new[shard] = jnp.where(alive, jnp.maximum(moved, 0.0), 0.0)
    for k in range(ntm - 1):
        new_copy(k).start()

    def all_step(step, carry):
        for piece in range(pieces):
            for w in range(2):
                all_copy(w, step - 1, piece).wait_recv()
                all_copy(w, step, piece).start()
                out_copy(w, step, piece).start()
        return carry

    lax.fori_loop(1, n - 1, all_step, 0)

    for k in range(ntm - 1):
        new_copy(k).wait()
    for o in range(ntm):
        pltpu.make_async_copy(
            rows_new.at[o], new_load_ref.at[pl.ds(o * span, span), :], rows_sem.at[o]
        ).start()

    for piece in range(pieces):
        for w in range(2):
            all_copy(w, n - 2, piece).wait_recv()
            out_copy(w, n - 1, piece).start()

    def drain(step, carry):
        for piece in range(pieces):
            for w in range(2):
                ring_copy(w, step, piece)[2].wait_send()
                all_copy(w, step, piece).wait_send()
                out_copy(w, step, piece).wait()
        norm_copy(step).wait_send()
        return carry

    lax.fori_loop(0, n - 1, drain, 0)
    for piece in range(pieces):
        for w in range(2):
            out_copy(w, n - 1, piece).wait()
    for o in range(ntm):
        pltpu.make_async_copy(
            rows_new.at[o], new_load_ref.at[pl.ds(o * span, span), :], rows_sem.at[o]
        ).wait()


def local(n, ntm, curves_data, loadings, profiles, counts):
    slots, points = curves_data.shape
    comps = loadings.shape[1]
    chunk = points // n
    sub = min(chunk, 256)
    pieces = 4
    half = comps // 2
    span = slots // ntm
    f32, bf16 = jnp.float32, jnp.bfloat16
    dma = pltpu.SemaphoreType.DMA
    flops = 3 * 3 * 2 * slots * points * comps
    return pl.pallas_call(
        functools.partial(kernel, n, ntm, pieces, sub),
        out_shape=(
            pltpu.VMEM((slots, comps), f32),
            pltpu.VMEM((points, comps), f32),
        ),
        in_specs=[
            pl.BlockSpec(memory_space=pltpu.SMEM),
            pl.BlockSpec(memory_space=pl.ANY),
            pl.BlockSpec(memory_space=pltpu.VMEM),
            pl.BlockSpec(memory_space=pl.ANY),
        ],
        out_specs=[pl.BlockSpec(memory_space=pltpu.VMEM)] * 2,
        scratch_shapes=[
            pltpu.VMEM((n, slots, chunk), f32),
            pltpu.VMEM((n, chunk, comps), f32),
            pltpu.VMEM((slots, comps), bf16),
            pltpu.VMEM((slots, comps), bf16),
            pltpu.VMEM((comps, slots), bf16),
            pltpu.VMEM((comps, slots), bf16),
            pltpu.VMEM((2, n, chunk, half), f32),
            pltpu.VMEM((2, n - 1, chunk, half), f32),
            pltpu.VMEM((2, n, chunk, half), f32),
            pltpu.VMEM((n, NORM_ROWS, comps), f32),
            pltpu.VMEM((ntm, span + NORM_ROWS, comps), f32),
            pltpu.VMEM((ntm - 1, span + NORM_ROWS, comps), f32),
            pltpu.VMEM((ntm, span, comps), f32),
            dma((n,)),
            dma((n,)),
            dma((2, n - 1, pieces)),
            dma((2, n - 1, pieces)),
            dma((2, n - 1, pieces)),
            dma((2, n - 1, pieces)),
            dma((n - 1,)),
            dma((n - 1,)),
            dma((ntm - 1,)),
            dma((ntm - 1,)),
            dma((ntm - 1,)),
            dma((ntm - 1,)),
            dma((2, n, pieces)),
            dma((ntm,)),
        ],
        compiler_params=pltpu.CompilerParams(
            collective_id=0, has_side_effects=True, vmem_limit_bytes=48 * 1024 * 1024
        ),
        cost_estimate=pl.CostEstimate(
            flops=flops, bytes_accessed=4 * (slots * points + 2 * points * comps), transcendentals=0
        ),
    )(counts, curves_data, loadings, profiles)


def solution(mesh):
    return jax.shard_map(
        functools.partial(local, mesh.shape["curves"], mesh.shape["tm"]),
        mesh=mesh,
        in_specs=(P("curves", "tm"), P("curves", None), P("tm", None), P()),
        out_specs=(P("curves", None), P("tm", None)),
        check_vma=False,
    )
```

```python
import functools

import jax
import jax.numpy as jnp
from jax import lax
from jax.experimental import pallas as pl
from jax.experimental.pallas import tpu as pltpu
from jax.sharding import PartitionSpec as P

MESH = pl.DeviceIdType.MESH
NORM_ROWS = 8


def split(value):
    high = value.astype(jnp.bfloat16)
    low = (value - high.astype(jnp.float32)).astype(jnp.bfloat16)
    return high, low


def left3(pair, axis):
    return jnp.concatenate((pair[0], pair[0], pair[1]), axis=axis)


def right3(pair, axis):
    return jnp.concatenate((pair[0], pair[1], pair[0]), axis=axis)


def dot(a, b, contract):
    return lax.dot_general(a, b, (contract, ((), ())), preferred_element_type=jnp.float32)


def kernel(
    n, ntm, pieces, sub,
    counts_hbm, data_ref, load_hbm, prof_ref,
    new_load_ref, new_prof_ref,
    counts_ref, load_ref, data_v, prof_v, load3, loadt3,
    grad, came, norms, rows_out, rows_in, rows_new,
    data_sem, prof_sem, ring_send, ring_recv, all_send, all_recv, norm_send, norm_recv,
    row_send, row_recv, new_send, new_recv, first_sem, rows_sem,
):
    slots, comps = load_ref.shape
    chunk = prof_v.shape[1]
    half = comps // 2
    part = chunk // pieces
    span = slots // ntm
    curve = lax.axis_index("curves")
    shard = lax.axis_index("tm")

    line = curve // 2
    me = jnp.where(curve % 2 == 0, line, n - 1 - line)

    def device_at(place):
        place = lax.rem(place + n, n)
        return jnp.where(place < n // 2, 2 * place, 2 * (n - 1 - place) + 1)

    ways = ((1, device_at(me + 1)), (-1, device_at(me - 1)))
    peers = [lax.rem(shard + k, ntm) for k in range(1, ntm)]

    first = (
        pltpu.make_async_copy(load_hbm, load_ref, first_sem.at[0]),
        pltpu.make_async_copy(counts_hbm, counts_ref, first_sem.at[1]),
    )
    for copy in first:
        copy.start()

    barrier = pltpu.get_barrier_semaphore()
    for _, other in ways:
        pl.semaphore_signal(barrier, inc=1, device_id={"curves": other}, device_id_type=MESH)
    for other in peers:
        pl.semaphore_signal(barrier, inc=1, device_id={"tm": other}, device_id_type=MESH)

    def chunk_at(order):
        step = (order + 1) // 2
        return lax.rem(jnp.where(order % 2 == 1, me - step, me + step) + n, n)

    def loads(order):
        c = chunk_at(order)
        start = pl.multiple_of(c * chunk, chunk)
        return (
            pltpu.make_async_copy(data_ref.at[:, pl.ds(start, chunk)], data_v.at[c], data_sem.at[c]),
            pltpu.make_async_copy(prof_ref.at[pl.ds(start, chunk), :], prof_v.at[c], prof_sem.at[c]),
        )

    def start_loads(order, carry):
        for copy in loads(order):
            copy.start()
        return carry

    lax.fori_loop(0, n, start_loads, 0)

    for copy in first:
        copy.wait()
    own = counts_ref[curve]
    keep = lax.broadcasted_iota(jnp.int32, (slots, 1), 0) < own
    load = load_ref[...]
    load3[...] = left3(split(load), 1)
    loadt3[...] = left3(split(load.T), 1)
    norm = jnp.sum(jnp.where(keep, load * load, 0.0), axis=0, keepdims=True)
    norms[me] = jnp.broadcast_to(norm, (NORM_ROWS, comps))
    rows_out[...] = jnp.zeros_like(rows_out)

    def compute(order, carry):
        c = chunk_at(order)
        for copy in loads(order):
            copy.wait()

        def piece(u, inner):
            start = pl.multiple_of(u * sub, sub)
            prof = prof_v[c, pl.ds(start, sub), :]
            prof2 = split(prof)
            recon = dot(load3[...], right3(prof2, 1), ((1,), (1,)))
            resid = jnp.where(keep, data_v[c, :, pl.ds(start, sub)] - recon, 0.0)
            resid2 = split(resid)
            row = dot(left3(resid2, 1), right3(prof2, 0), ((1,), (0,)))
            square = jnp.broadcast_to(jnp.sum(prof * prof, axis=0, keepdims=True), (NORM_ROWS, comps))
            for o in range(ntm):
                rows_out[o, :span, :] += row[o * span:(o + 1) * span]
                rows_out[o, span:, :] += square
            time = dot(loadt3[...], right3(resid2, 0), ((1,), (0,))).T
            grad[0, c, pl.ds(start, sub), :] = time[:, :half]
            grad[1, c, pl.ds(start, sub), :] = time[:, half:]
            return inner

        lax.fori_loop(0, chunk // sub, piece, 0)
        return carry

    def row_copy(k):
        other = peers[k]
        return pltpu.make_async_remote_copy(
            src_ref=rows_out.at[other], dst_ref=rows_in.at[k],
            send_sem=row_send.at[k], recv_sem=row_recv.at[k],
            device_id={"tm": other}, device_id_type=MESH,
        )

    def new_copy(k):
        return pltpu.make_async_remote_copy(
            src_ref=rows_new.at[shard], dst_ref=rows_new.at[shard],
            send_sem=new_send.at[k], recv_sem=new_recv.at[k],
            device_id={"tm": peers[k]}, device_id_type=MESH,
        )

    def ring_copy(w, step, piece):
        sign, other = ways[w]
        c = lax.rem(me - sign * step + 2 * n, n)
        at = pl.ds(piece * part, part)
        return c, at, pltpu.make_async_remote_copy(
            src_ref=grad.at[w, c, at, :], dst_ref=came.at[w, step, at, :],
            send_sem=ring_send.at[w, step, piece], recv_sem=ring_recv.at[w, step, piece],
            device_id={"curves": other}, device_id_type=MESH,
        )

    def norm_copy(step):
        c = lax.rem(me - step + 2 * n, n)
        return pltpu.make_async_remote_copy(
            src_ref=norms.at[c], dst_ref=norms.at[c],
            send_sem=norm_send.at[step], recv_sem=norm_recv.at[step],
            device_id={"curves": ways[0][1]}, device_id_type=MESH,
        )

    def place(w, c, piece):
        rows = pl.ds(pl.multiple_of(c * chunk + piece * part, part), part)
        return new_prof_ref.at[rows, pl.ds(w * half, half)]

    def all_copy(w, step, piece):
        sign, other = ways[w]
        c = lax.rem(me + sign - sign * step + 2 * n, n)
        return pltpu.make_async_remote_copy(
            src_ref=place(w, c, piece), dst_ref=place(w, c, piece),
            send_sem=all_send.at[w, step, piece], recv_sem=all_recv.at[w, step, piece],
            device_id={"curves": other}, device_id_type=MESH,
        )

    pl.semaphore_wait(barrier, 2 + len(peers))

    def ring_step(step, carry):
        for w in range(2):
            lo = jnp.maximum(2 * step + w - 1, w)
            hi = jnp.minimum(jnp.maximum(2 * step + w, 1), n)
            lax.fori_loop(lo, hi, compute, 0)

            for piece in range(pieces):
                c, at, copy = ring_copy(w, step, piece)

                @pl.when(step > 0)
                def _():
                    ring_copy(w, step - 1, piece)[2].wait_recv()
                    grad[w, c, at, :] = grad[w, c, at, :] + came[w, step - 1, at, :]

                copy.start()

        @pl.when(step == n // 2)
        def _():
            for k in range(ntm - 1):
                row_copy(k).start()

        @pl.when(step > 0)
        def _():
            norm_copy(step - 1).wait_recv()

        norm_copy(step).start()
        return carry

    lax.fori_loop(0, n - 1, ring_step, 0)

    norm_copy(n - 2).wait_recv()
    total = norms[0]
    for k in range(1, n):
        total = total + norms[k]
    total = total[0:1]

    for piece in range(pieces):
        for w in range(2):
            ring_copy(w, n - 2, piece)[2].wait_recv()
            sign, _ = ways[w]
            c = lax.rem(me + sign + n, n)
            at = pl.ds(piece * part, part)
            lanes = pl.ds(w * half, half)
            summed = grad[w, c, at, :] + came[w, n - 2, at, :]
            place(w, c, piece)[...] = jnp.maximum(
                prof_v[c, at, lanes] + summed / total[:, w * half:(w + 1) * half], 0.0
            )
            all_copy(w, 0, piece).start()

    for k in range(ntm - 1):
        row_copy(k).wait()
    mine = rows_out[shard]
    for k in range(ntm - 1):
        mine = mine + rows_in[k]
    base = pl.multiple_of(shard * span, span)
    alive = base + lax.broadcasted_iota(jnp.int32, (span, 1), 0) < own
    moved = load_ref[pl.ds(base, span), :] + mine[:span] / mine[span:span + 1]
    rows_new[shard] = jnp.where(alive, jnp.maximum(moved, 0.0), 0.0)
    for k in range(ntm - 1):
        new_copy(k).start()

    def all_step(step, carry):
        for piece in range(pieces):
            for w in range(2):
                all_copy(w, step - 1, piece).wait_recv()
                all_copy(w, step, piece).start()
        return carry

    lax.fori_loop(1, n - 1, all_step, 0)

    for k in range(ntm - 1):
        new_copy(k).wait()
    for o in range(ntm):
        pltpu.make_async_copy(
            rows_new.at[o], new_load_ref.at[pl.ds(o * span, span), :], rows_sem.at[o]
        ).start()

    for piece in range(pieces):
        for w in range(2):
            all_copy(w, n - 2, piece).wait_recv()

    def drain(step, carry):
        for piece in range(pieces):
            for w in range(2):
                ring_copy(w, step, piece)[2].wait_send()
                all_copy(w, step, piece).wait_send()
        norm_copy(step).wait_send()
        return carry

    lax.fori_loop(0, n - 1, drain, 0)
    for o in range(ntm):
        pltpu.make_async_copy(
            rows_new.at[o], new_load_ref.at[pl.ds(o * span, span), :], rows_sem.at[o]
        ).wait()


def local(n, ntm, curves_data, loadings, profiles, counts):
    slots, points = curves_data.shape
    comps = loadings.shape[1]
    chunk = points // n
    sub = min(chunk, 512)
    pieces = 4
    half = comps // 2
    span = slots // ntm
    f32, bf16 = jnp.float32, jnp.bfloat16
    dma = pltpu.SemaphoreType.DMA
    flops = 3 * 3 * 2 * slots * points * comps
    return pl.pallas_call(
        functools.partial(kernel, n, ntm, pieces, sub),
        out_shape=(
            pltpu.VMEM((slots, comps), f32),
            pltpu.VMEM((points, comps), f32),
        ),
        in_specs=[pl.BlockSpec(memory_space=pltpu.HBM)] * 4,
        out_specs=[pl.BlockSpec(memory_space=pltpu.VMEM)] * 2,
        scratch_shapes=[
            pltpu.SMEM((n,), jnp.int32),
            pltpu.VMEM((slots, comps), f32),
            pltpu.VMEM((n, slots, chunk), f32),
            pltpu.VMEM((n, chunk, comps), f32),
            pltpu.VMEM((slots, 3 * comps), bf16),
            pltpu.VMEM((comps, 3 * slots), bf16),
            pltpu.VMEM((2, n, chunk, half), f32),
            pltpu.VMEM((2, n - 1, chunk, half), f32),
            pltpu.VMEM((n, NORM_ROWS, comps), f32),
            pltpu.VMEM((ntm, span + NORM_ROWS, comps), f32),
            pltpu.VMEM((ntm - 1, span + NORM_ROWS, comps), f32),
            pltpu.VMEM((ntm, span, comps), f32),
            dma((n,)),
            dma((n,)),
            dma((2, n - 1, pieces)),
            dma((2, n - 1, pieces)),
            dma((2, n - 1, pieces)),
            dma((2, n - 1, pieces)),
            dma((n - 1,)),
            dma((n - 1,)),
            dma((ntm - 1,)),
            dma((ntm - 1,)),
            dma((ntm - 1,)),
            dma((ntm - 1,)),
            dma((2,)),
            dma((ntm,)),
        ],
        compiler_params=pltpu.CompilerParams(
            collective_id=0, has_side_effects=True, vmem_limit_bytes=48 * 1024 * 1024
        ),
        cost_estimate=pl.CostEstimate(
            flops=flops, bytes_accessed=4 * (slots * points + 2 * points * comps), transcendentals=0
        ),
    )(counts, curves_data, loadings, profiles)


def solution(mesh):
    return jax.shard_map(
        functools.partial(local, mesh.shape["curves"], mesh.shape["tm"]),
        mesh=mesh,
        in_specs=(P("curves", "tm"), P("curves", None), P("tm", None), P()),
        out_specs=(P("curves", None), P("tm", None)),
        check_vma=False,
    )
```

```python
import functools

import jax
import jax.numpy as jnp
from jax import lax
from jax.experimental import pallas as pl
from jax.experimental.pallas import tpu as pltpu
from jax.sharding import PartitionSpec as P

MESH = pl.DeviceIdType.MESH
NORM_ROWS = 8


def split(value):
    high = value.astype(jnp.bfloat16)
    low = (value - high.astype(jnp.float32)).astype(jnp.bfloat16)
    return high, low


def left3(pair, axis):
    return jnp.concatenate((pair[0], pair[0], pair[1]), axis=axis)


def right3(pair, axis):
    return jnp.concatenate((pair[0], pair[1], pair[0]), axis=axis)


def dot(a, b, contract):
    return lax.dot_general(a, b, (contract, ((), ())), preferred_element_type=jnp.float32)


def kernel(
    n, ntm, pieces, sub,
    counts_hbm, data_ref, load_hbm, prof_ref,
    new_load_ref, new_prof_ref,
    counts_ref, load_ref, data_v, prof_v, load3, loadt3,
    grad, came, norms, rows_out, rows_in, rows_new,
    data_sem, prof_sem, ring_send, ring_recv, all_send, all_recv, norm_send, norm_recv,
    row_send, row_recv, new_send, new_recv, first_sem, rows_sem,
):
    slots, comps = load_ref.shape
    chunk = prof_v.shape[1]
    half = comps // 2
    part = chunk // pieces
    span = slots // ntm
    curve = lax.axis_index("curves")
    shard = lax.axis_index("tm")

    line = curve // 2
    me = jnp.where(curve % 2 == 0, line, n - 1 - line)

    def device_at(place):
        place = lax.rem(place + n, n)
        return jnp.where(place < n // 2, 2 * place, 2 * (n - 1 - place) + 1)

    ways = ((1, device_at(me + 1)), (-1, device_at(me - 1)))
    peers = [lax.rem(shard + k, ntm) for k in range(1, ntm)]

    first = (
        pltpu.make_async_copy(load_hbm, load_ref, first_sem.at[0]),
        pltpu.make_async_copy(counts_hbm, counts_ref, first_sem.at[1]),
    )
    for copy in first:
        copy.start()

    barrier = pltpu.get_barrier_semaphore()
    for _, other in ways:
        pl.semaphore_signal(barrier, inc=1, device_id={"curves": other}, device_id_type=MESH)
    for other in peers:
        pl.semaphore_signal(barrier, inc=1, device_id={"tm": other}, device_id_type=MESH)

    def chunk_at(order):
        step = (order + 1) // 2
        return lax.rem(jnp.where(order % 2 == 1, me - step, me + step) + n, n)

    def loads(order):
        c = chunk_at(order)
        start = pl.multiple_of(c * chunk, chunk)
        return (
            pltpu.make_async_copy(data_ref.at[:, pl.ds(start, chunk)], data_v.at[c], data_sem.at[c]),
            pltpu.make_async_copy(prof_ref.at[pl.ds(start, chunk), :], prof_v.at[c], prof_sem.at[c]),
        )

    def start_loads(order, carry):
        for copy in loads(order):
            copy.start()
        return carry

    start_loads(0, 0)
    for copy in first:
        copy.wait()
    lax.fori_loop(1, n, start_loads, 0)
    own = counts_ref[curve]
    keep = lax.broadcasted_iota(jnp.int32, (slots, 1), 0) < own
    load = load_ref[...]
    load3[...] = left3(split(load), 1)
    loadt3[...] = left3(split(load.T), 1)
    norm = jnp.sum(jnp.where(keep, load * load, 0.0), axis=0, keepdims=True)
    norms[me] = jnp.broadcast_to(norm, (NORM_ROWS, comps))
    rows_out[...] = jnp.zeros_like(rows_out)

    def compute(order, carry):
        c = chunk_at(order)
        for copy in loads(order):
            copy.wait()

        def piece(u, inner):
            start = pl.multiple_of(u * sub, sub)
            prof = prof_v[c, pl.ds(start, sub), :]
            prof2 = split(prof)
            recon = dot(load3[...], right3(prof2, 1), ((1,), (1,)))
            resid = jnp.where(keep, data_v[c, :, pl.ds(start, sub)] - recon, 0.0)
            resid2 = split(resid)
            row = dot(left3(resid2, 1), right3(prof2, 0), ((1,), (0,)))
            square = jnp.broadcast_to(jnp.sum(prof * prof, axis=0, keepdims=True), (NORM_ROWS, comps))
            for o in range(ntm):
                rows_out[o, :span, :] += row[o * span:(o + 1) * span]
                rows_out[o, span:, :] += square
            time = dot(loadt3[...], right3(resid2, 0), ((1,), (0,))).T
            grad[0, c, pl.ds(start, sub), :] = time[:, :half]
            grad[1, c, pl.ds(start, sub), :] = time[:, half:]
            return inner

        lax.fori_loop(0, chunk // sub, piece, 0)
        return carry

    def row_copy(k):
        other = peers[k]
        return pltpu.make_async_remote_copy(
            src_ref=rows_out.at[other], dst_ref=rows_in.at[k],
            send_sem=row_send.at[k], recv_sem=row_recv.at[k],
            device_id={"tm": other}, device_id_type=MESH,
        )

    def new_copy(k):
        return pltpu.make_async_remote_copy(
            src_ref=rows_new.at[shard], dst_ref=rows_new.at[shard],
            send_sem=new_send.at[k], recv_sem=new_recv.at[k],
            device_id={"tm": peers[k]}, device_id_type=MESH,
        )

    def ring_copy(w, step, piece):
        sign, other = ways[w]
        c = lax.rem(me - sign * step + 2 * n, n)
        at = pl.ds(piece * part, part)
        return c, at, pltpu.make_async_remote_copy(
            src_ref=grad.at[w, c, at, :], dst_ref=came.at[w, step, at, :],
            send_sem=ring_send.at[w, step, piece], recv_sem=ring_recv.at[w, step, piece],
            device_id={"curves": other}, device_id_type=MESH,
        )

    def norm_copy(step):
        c = lax.rem(me - step + 2 * n, n)
        return pltpu.make_async_remote_copy(
            src_ref=norms.at[c], dst_ref=norms.at[c],
            send_sem=norm_send.at[step], recv_sem=norm_recv.at[step],
            device_id={"curves": ways[0][1]}, device_id_type=MESH,
        )

    def place(w, c, piece):
        rows = pl.ds(pl.multiple_of(c * chunk + piece * part, part), part)
        return new_prof_ref.at[rows, pl.ds(w * half, half)]

    def all_copy(w, step, piece):
        sign, other = ways[w]
        c = lax.rem(me + sign - sign * step + 2 * n, n)
        return pltpu.make_async_remote_copy(
            src_ref=place(w, c, piece), dst_ref=place(w, c, piece),
            send_sem=all_send.at[w, step, piece], recv_sem=all_recv.at[w, step, piece],
            device_id={"curves": other}, device_id_type=MESH,
        )

    lax.fori_loop(0, 1, compute, 0)
    pl.semaphore_wait(barrier, 2 + len(peers))

    def ring_step(step, carry):
        for w in range(2):
            lo = jnp.maximum(2 * step + w - 1, 1)
            hi = jnp.minimum(2 * step + w, n)
            lax.fori_loop(lo, hi, compute, 0)

            for piece in range(pieces):
                c, at, copy = ring_copy(w, step, piece)

                @pl.when(step > 0)
                def _():
                    ring_copy(w, step - 1, piece)[2].wait_recv()
                    grad[w, c, at, :] = grad[w, c, at, :] + came[w, step - 1, at, :]

                copy.start()

        @pl.when(step == n // 2)
        def _():
            for k in range(ntm - 1):
                row_copy(k).start()

        @pl.when(step > 0)
        def _():
            norm_copy(step - 1).wait_recv()

        norm_copy(step).start()
        return carry

    lax.fori_loop(0, n - 1, ring_step, 0)

    norm_copy(n - 2).wait_recv()
    total = norms[0]
    for k in range(1, n):
        total = total + norms[k]
    total = total[0:1]

    for piece in range(pieces):
        for w in range(2):
            ring_copy(w, n - 2, piece)[2].wait_recv()
            sign, _ = ways[w]
            c = lax.rem(me + sign + n, n)
            at = pl.ds(piece * part, part)
            lanes = pl.ds(w * half, half)
            summed = grad[w, c, at, :] + came[w, n - 2, at, :]
            place(w, c, piece)[...] = jnp.maximum(
                prof_v[c, at, lanes] + summed / total[:, w * half:(w + 1) * half], 0.0
            )
            all_copy(w, 0, piece).start()

    for k in range(ntm - 1):
        row_copy(k).wait()
    mine = rows_out[shard]
    for k in range(ntm - 1):
        mine = mine + rows_in[k]
    base = pl.multiple_of(shard * span, span)
    alive = base + lax.broadcasted_iota(jnp.int32, (span, 1), 0) < own
    moved = load_ref[pl.ds(base, span), :] + mine[:span] / mine[span:span + 1]
    rows_new[shard] = jnp.where(alive, jnp.maximum(moved, 0.0), 0.0)
    for k in range(ntm - 1):
        new_copy(k).start()

    def all_step(step, carry):
        for piece in range(pieces):
            for w in range(2):
                all_copy(w, step - 1, piece).wait_recv()
                all_copy(w, step, piece).start()
        return carry

    lax.fori_loop(1, n - 1, all_step, 0)

    for k in range(ntm - 1):
        new_copy(k).wait()
    for o in range(ntm):
        pltpu.make_async_copy(
            rows_new.at[o], new_load_ref.at[pl.ds(o * span, span), :], rows_sem.at[o]
        ).start()

    for piece in range(pieces):
        for w in range(2):
            all_copy(w, n - 2, piece).wait_recv()

    def drain(step, carry):
        for piece in range(pieces):
            for w in range(2):
                ring_copy(w, step, piece)[2].wait_send()
                all_copy(w, step, piece).wait_send()
        norm_copy(step).wait_send()
        return carry

    lax.fori_loop(0, n - 1, drain, 0)
    for o in range(ntm):
        pltpu.make_async_copy(
            rows_new.at[o], new_load_ref.at[pl.ds(o * span, span), :], rows_sem.at[o]
        ).wait()


def local(n, ntm, curves_data, loadings, profiles, counts):
    slots, points = curves_data.shape
    comps = loadings.shape[1]
    chunk = points // n
    sub = min(chunk, 512)
    pieces = 4
    half = comps // 2
    span = slots // ntm
    f32, bf16 = jnp.float32, jnp.bfloat16
    dma = pltpu.SemaphoreType.DMA
    flops = 3 * 3 * 2 * slots * points * comps
    return pl.pallas_call(
        functools.partial(kernel, n, ntm, pieces, sub),
        out_shape=(
            pltpu.VMEM((slots, comps), f32),
            pltpu.VMEM((points, comps), f32),
        ),
        in_specs=[pl.BlockSpec(memory_space=pltpu.HBM)] * 4,
        out_specs=[pl.BlockSpec(memory_space=pltpu.VMEM)] * 2,
        scratch_shapes=[
            pltpu.SMEM((n,), jnp.int32),
            pltpu.VMEM((slots, comps), f32),
            pltpu.VMEM((n, slots, chunk), f32),
            pltpu.VMEM((n, chunk, comps), f32),
            pltpu.VMEM((slots, 3 * comps), bf16),
            pltpu.VMEM((comps, 3 * slots), bf16),
            pltpu.VMEM((2, n, chunk, half), f32),
            pltpu.VMEM((2, n - 1, chunk, half), f32),
            pltpu.VMEM((n, NORM_ROWS, comps), f32),
            pltpu.VMEM((ntm, span + NORM_ROWS, comps), f32),
            pltpu.VMEM((ntm - 1, span + NORM_ROWS, comps), f32),
            pltpu.VMEM((ntm, span, comps), f32),
            dma((n,)),
            dma((n,)),
            dma((2, n - 1, pieces)),
            dma((2, n - 1, pieces)),
            dma((2, n - 1, pieces)),
            dma((2, n - 1, pieces)),
            dma((n - 1,)),
            dma((n - 1,)),
            dma((ntm - 1,)),
            dma((ntm - 1,)),
            dma((ntm - 1,)),
            dma((ntm - 1,)),
            dma((2,)),
            dma((ntm,)),
        ],
        compiler_params=pltpu.CompilerParams(
            collective_id=0, has_side_effects=True, vmem_limit_bytes=58 * 1024 * 1024
        ),
        cost_estimate=pl.CostEstimate(
            flops=flops, bytes_accessed=4 * (slots * points + 2 * points * comps), transcendentals=0
        ),
    )(counts, curves_data, loadings, profiles)


def solution(mesh):
    return jax.shard_map(
        functools.partial(local, mesh.shape["curves"], mesh.shape["tm"]),
        mesh=mesh,
        in_specs=(P("curves", "tm"), P("curves", None), P("tm", None), P()),
        out_specs=(P("curves", None), P("tm", None)),
        check_vma=False,
    )
```

```python
import functools

import jax
import jax.numpy as jnp
from jax import lax
from jax.experimental import pallas as pl
from jax.experimental.pallas import tpu as pltpu
from jax.sharding import PartitionSpec as P

MESH = pl.DeviceIdType.MESH
NORM_ROWS = 8


def split(value):
    high = value.astype(jnp.bfloat16)
    low = (value - high.astype(jnp.float32)).astype(jnp.bfloat16)
    return high, low


def left3(pair, axis):
    return jnp.concatenate((pair[0], pair[0], pair[1]), axis=axis)


def right3(pair, axis):
    return jnp.concatenate((pair[0], pair[1], pair[0]), axis=axis)


def dot(a, b, contract):
    return lax.dot_general(a, b, (contract, ((), ())), preferred_element_type=jnp.float32)


def kernel(
    n, ntm, pieces, sub,
    counts_hbm, data_ref, load_hbm, prof_ref,
    new_load_ref, new_prof_ref,
    counts_ref, load_ref, data_v, prof_v, load3, loadt3,
    grad, came, norms, rows_out, rows_in, rows_new,
    data_sem, prof_sem, ring_send, ring_recv, all_send, all_recv, norm_send, norm_recv,
    row_send, row_recv, new_send, new_recv, first_sem, rows_sem,
):
    slots, comps = load_ref.shape
    chunk = prof_v.shape[1]
    half = comps // 2
    part = chunk // pieces
    span = slots // ntm
    curve = lax.axis_index("curves")
    shard = lax.axis_index("tm")

    line = curve // 2
    me = jnp.where(curve % 2 == 0, line, n - 1 - line)

    def device_at(place):
        place = lax.rem(place + n, n)
        return jnp.where(place < n // 2, 2 * place, 2 * (n - 1 - place) + 1)

    ways = ((1, device_at(me + 1)), (-1, device_at(me - 1)))
    peers = [lax.rem(shard + k, ntm) for k in range(1, ntm)]

    first = (
        pltpu.make_async_copy(load_hbm, load_ref, first_sem.at[0]),
        pltpu.make_async_copy(counts_hbm, counts_ref, first_sem.at[1]),
    )
    for copy in first:
        copy.start()

    barrier = pltpu.get_barrier_semaphore()
    for _, other in ways:
        pl.semaphore_signal(barrier, inc=1, device_id={"curves": other}, device_id_type=MESH)
    for other in peers:
        pl.semaphore_signal(barrier, inc=1, device_id={"tm": other}, device_id_type=MESH)

    def chunk_at(order):
        step = (order + 1) // 2
        return lax.rem(jnp.where(order % 2 == 1, me - step, me + step) + n, n)

    def loads(order):
        c = chunk_at(order)
        start = pl.multiple_of(c * chunk, chunk)
        return (
            pltpu.make_async_copy(data_ref.at[:, pl.ds(start, chunk)], data_v.at[c], data_sem.at[c]),
            pltpu.make_async_copy(prof_ref.at[pl.ds(start, chunk), :], prof_v.at[c], prof_sem.at[c]),
        )

    def start_loads(order, carry):
        for copy in loads(order):
            copy.start()
        return carry

    start_loads(0, 0)
    for copy in first:
        copy.wait()
    lax.fori_loop(1, n, start_loads, 0)
    own = counts_ref[curve]
    keep = lax.broadcasted_iota(jnp.int32, (slots, 1), 0) < own
    load = load_ref[...]
    load3[...] = left3(split(load), 1)
    loadt3[...] = left3(split(load.T), 1)
    norm = jnp.sum(jnp.where(keep, load * load, 0.0), axis=0, keepdims=True)
    norms[me] = jnp.broadcast_to(norm, (NORM_ROWS, comps))
    rows_out[...] = jnp.zeros_like(rows_out)

    def compute(order, carry):
        c = chunk_at(order)
        for copy in loads(order):
            copy.wait()

        def piece(u, inner):
            start = pl.multiple_of(u * sub, sub)
            prof = prof_v[c, pl.ds(start, sub), :]
            prof2 = split(prof)
            recon = dot(load3[...], right3(prof2, 1), ((1,), (1,)))
            resid = jnp.where(keep, data_v[c, :, pl.ds(start, sub)] - recon, 0.0)
            data_v[c, :, pl.ds(start, sub)] = resid
            time = dot(loadt3[...], right3(split(resid), 0), ((1,), (0,))).T
            grad[0, c, pl.ds(start, sub), :] = time[:, :half]
            grad[1, c, pl.ds(start, sub), :] = time[:, half:]
            return inner

        lax.fori_loop(0, chunk // sub, piece, 0)
        return carry

    def row_terms(order, carry):
        c = chunk_at(order)
        prof = prof_v[c]
        row = dot(left3(split(data_v[c]), 1), right3(split(prof), 0), ((1,), (0,)))
        square = jnp.broadcast_to(jnp.sum(prof * prof, axis=0, keepdims=True), (NORM_ROWS, comps))
        for o in range(ntm):
            rows_out[o, :span, :] += row[o * span:(o + 1) * span]
            rows_out[o, span:, :] += square
        return carry

    def row_copy(k):
        other = peers[k]
        return pltpu.make_async_remote_copy(
            src_ref=rows_out.at[other], dst_ref=rows_in.at[k],
            send_sem=row_send.at[k], recv_sem=row_recv.at[k],
            device_id={"tm": other}, device_id_type=MESH,
        )

    def new_copy(k):
        return pltpu.make_async_remote_copy(
            src_ref=rows_new.at[shard], dst_ref=rows_new.at[shard],
            send_sem=new_send.at[k], recv_sem=new_recv.at[k],
            device_id={"tm": peers[k]}, device_id_type=MESH,
        )

    def ring_copy(w, step, piece):
        sign, other = ways[w]
        c = lax.rem(me - sign * step + 2 * n, n)
        at = pl.ds(piece * part, part)
        return c, at, pltpu.make_async_remote_copy(
            src_ref=grad.at[w, c, at, :], dst_ref=came.at[w, step, at, :],
            send_sem=ring_send.at[w, step, piece], recv_sem=ring_recv.at[w, step, piece],
            device_id={"curves": other}, device_id_type=MESH,
        )

    def norm_copy(step):
        c = lax.rem(me - step + 2 * n, n)
        return pltpu.make_async_remote_copy(
            src_ref=norms.at[c], dst_ref=norms.at[c],
            send_sem=norm_send.at[step], recv_sem=norm_recv.at[step],
            device_id={"curves": ways[0][1]}, device_id_type=MESH,
        )

    def place(w, c, piece):
        rows = pl.ds(pl.multiple_of(c * chunk + piece * part, part), part)
        return new_prof_ref.at[rows, pl.ds(w * half, half)]

    def all_copy(w, step, piece):
        sign, other = ways[w]
        c = lax.rem(me + sign - sign * step + 2 * n, n)
        return pltpu.make_async_remote_copy(
            src_ref=place(w, c, piece), dst_ref=place(w, c, piece),
            send_sem=all_send.at[w, step, piece], recv_sem=all_recv.at[w, step, piece],
            device_id={"curves": other}, device_id_type=MESH,
        )

    lax.fori_loop(0, 1, compute, 0)
    pl.semaphore_wait(barrier, 2 + len(peers))

    def ring_step(step, carry):
        for w in range(2):
            lo = jnp.maximum(2 * step + w - 1, 1)
            hi = jnp.minimum(2 * step + w, n)
            lax.fori_loop(lo, hi, compute, 0)
            late = 2 * step + w - n
            lax.fori_loop(jnp.maximum(late, 0), jnp.maximum(late + 1, 0), row_terms, 0)

            for piece in range(pieces):
                c, at, copy = ring_copy(w, step, piece)

                @pl.when(step > 0)
                def _():
                    ring_copy(w, step - 1, piece)[2].wait_recv()
                    grad[w, c, at, :] = grad[w, c, at, :] + came[w, step - 1, at, :]

                copy.start()

        @pl.when(step > 0)
        def _():
            norm_copy(step - 1).wait_recv()

        norm_copy(step).start()
        return carry

    lax.fori_loop(0, n - 1, ring_step, 0)

    norm_copy(n - 2).wait_recv()
    total = norms[0]
    for k in range(1, n):
        total = total + norms[k]
    total = total[0:1]

    for piece in range(pieces):
        for w in range(2):
            ring_copy(w, n - 2, piece)[2].wait_recv()
            sign, _ = ways[w]
            c = lax.rem(me + sign + n, n)
            at = pl.ds(piece * part, part)
            lanes = pl.ds(w * half, half)
            summed = grad[w, c, at, :] + came[w, n - 2, at, :]
            place(w, c, piece)[...] = jnp.maximum(
                prof_v[c, at, lanes] + summed / total[:, w * half:(w + 1) * half], 0.0
            )
            all_copy(w, 0, piece).start()

    lax.fori_loop(n - 2, n, row_terms, 0)
    for k in range(ntm - 1):
        row_copy(k).start()

    def share_rows():
        for k in range(ntm - 1):
            row_copy(k).wait()
        mine = rows_out[shard]
        for k in range(ntm - 1):
            mine = mine + rows_in[k]
        base = pl.multiple_of(shard * span, span)
        alive = base + lax.broadcasted_iota(jnp.int32, (span, 1), 0) < own
        moved = load_ref[pl.ds(base, span), :] + mine[:span] / mine[span:span + 1]
        rows_new[shard] = jnp.where(alive, jnp.maximum(moved, 0.0), 0.0)
        for k in range(ntm - 1):
            new_copy(k).start()

    def all_step(step, carry):
        for piece in range(pieces):
            for w in range(2):
                all_copy(w, step - 1, piece).wait_recv()
                all_copy(w, step, piece).start()
        pl.when(step == n // 2)(share_rows)
        return carry

    lax.fori_loop(1, n - 1, all_step, 0)

    for k in range(ntm - 1):
        new_copy(k).wait()
    for o in range(ntm):
        pltpu.make_async_copy(
            rows_new.at[o], new_load_ref.at[pl.ds(o * span, span), :], rows_sem.at[o]
        ).start()

    for piece in range(pieces):
        for w in range(2):
            all_copy(w, n - 2, piece).wait_recv()

    def drain(step, carry):
        for piece in range(pieces):
            for w in range(2):
                ring_copy(w, step, piece)[2].wait_send()
                all_copy(w, step, piece).wait_send()
        norm_copy(step).wait_send()
        return carry

    lax.fori_loop(0, n - 1, drain, 0)
    for o in range(ntm):
        pltpu.make_async_copy(
            rows_new.at[o], new_load_ref.at[pl.ds(o * span, span), :], rows_sem.at[o]
        ).wait()


def local(n, ntm, curves_data, loadings, profiles, counts):
    slots, points = curves_data.shape
    comps = loadings.shape[1]
    chunk = points // n
    sub = min(chunk, 512)
    pieces = 4
    half = comps // 2
    span = slots // ntm
    f32, bf16 = jnp.float32, jnp.bfloat16
    dma = pltpu.SemaphoreType.DMA
    flops = 3 * 3 * 2 * slots * points * comps
    return pl.pallas_call(
        functools.partial(kernel, n, ntm, pieces, sub),
        out_shape=(
            pltpu.VMEM((slots, comps), f32),
            pltpu.VMEM((points, comps), f32),
        ),
        in_specs=[pl.BlockSpec(memory_space=pltpu.HBM)] * 4,
        out_specs=[pl.BlockSpec(memory_space=pltpu.VMEM)] * 2,
        scratch_shapes=[
            pltpu.SMEM((n,), jnp.int32),
            pltpu.VMEM((slots, comps), f32),
            pltpu.VMEM((n, slots, chunk), f32),
            pltpu.VMEM((n, chunk, comps), f32),
            pltpu.VMEM((slots, 3 * comps), bf16),
            pltpu.VMEM((comps, 3 * slots), bf16),
            pltpu.VMEM((2, n, chunk, half), f32),
            pltpu.VMEM((2, n - 1, chunk, half), f32),
            pltpu.VMEM((n, NORM_ROWS, comps), f32),
            pltpu.VMEM((ntm, span + NORM_ROWS, comps), f32),
            pltpu.VMEM((ntm - 1, span + NORM_ROWS, comps), f32),
            pltpu.VMEM((ntm, span, comps), f32),
            dma((n,)),
            dma((n,)),
            dma((2, n - 1, pieces)),
            dma((2, n - 1, pieces)),
            dma((2, n - 1, pieces)),
            dma((2, n - 1, pieces)),
            dma((n - 1,)),
            dma((n - 1,)),
            dma((ntm - 1,)),
            dma((ntm - 1,)),
            dma((ntm - 1,)),
            dma((ntm - 1,)),
            dma((2,)),
            dma((ntm,)),
        ],
        compiler_params=pltpu.CompilerParams(
            collective_id=0, has_side_effects=True, vmem_limit_bytes=58 * 1024 * 1024
        ),
        cost_estimate=pl.CostEstimate(
            flops=flops, bytes_accessed=4 * (slots * points + 2 * points * comps), transcendentals=0
        ),
    )(counts, curves_data, loadings, profiles)


def solution(mesh):
    return jax.shard_map(
        functools.partial(local, mesh.shape["curves"], mesh.shape["tm"]),
        mesh=mesh,
        in_specs=(P("curves", "tm"), P("curves", None), P("tm", None), P()),
        out_specs=(P("curves", None), P("tm", None)),
        check_vma=False,
    )
```

```python
import functools

import jax
import jax.numpy as jnp
from jax import lax
from jax.experimental import pallas as pl
from jax.experimental.pallas import tpu as pltpu
from jax.sharding import PartitionSpec as P

MESH = pl.DeviceIdType.MESH
NORM_ROWS = 8


def split(value):
    high = value.astype(jnp.bfloat16)
    low = (value - high.astype(jnp.float32)).astype(jnp.bfloat16)
    return high, low


def left3(pair, axis):
    return jnp.concatenate((pair[0], pair[0], pair[1]), axis=axis)


def right3(pair, axis):
    return jnp.concatenate((pair[0], pair[1], pair[0]), axis=axis)


def dot(a, b, contract):
    return lax.dot_general(a, b, (contract, ((), ())), preferred_element_type=jnp.float32)


def kernel(
    n, ntm, pieces, sub,
    counts_hbm, data_ref, load_hbm, prof_ref,
    new_load_ref, new_prof_ref,
    counts_ref, load_ref, data_v, prof_v, load3, loadt3,
    grad, came, norms, rows_out, rows_in, rows_new,
    data_sem, prof_sem, ring_send, ring_recv, all_send, all_recv, norm_send, norm_recv,
    row_send, row_recv, new_send, new_recv, first_sem, rows_sem,
):
    slots, comps = load_ref.shape
    chunk = prof_v.shape[1]
    half = comps // 2
    part = chunk // pieces
    span = slots // ntm
    curve = lax.axis_index("curves")
    shard = lax.axis_index("tm")

    line = curve // 2
    me = jnp.where(curve % 2 == 0, line, n - 1 - line)

    def device_at(place):
        place = lax.rem(place + n, n)
        return jnp.where(place < n // 2, 2 * place, 2 * (n - 1 - place) + 1)

    ways = ((1, device_at(me + 1)), (-1, device_at(me - 1)))
    peers = [lax.rem(shard + k, ntm) for k in range(1, ntm)]

    first = (
        pltpu.make_async_copy(load_hbm, load_ref, first_sem.at[0]),
        pltpu.make_async_copy(counts_hbm, counts_ref, first_sem.at[1]),
    )
    for copy in first:
        copy.start()

    barrier = pltpu.get_barrier_semaphore()
    for _, other in ways:
        pl.semaphore_signal(barrier, inc=1, device_id={"curves": other}, device_id_type=MESH)
    for other in peers:
        pl.semaphore_signal(barrier, inc=1, device_id={"tm": other}, device_id_type=MESH)

    def chunk_at(order):
        step = (order + 1) // 2
        return lax.rem(jnp.where(order % 2 == 1, me - step, me + step) + n, n)

    def loads(order):
        c = chunk_at(order)
        start = pl.multiple_of(c * chunk, chunk)
        return (
            pltpu.make_async_copy(data_ref.at[:, pl.ds(start, chunk)], data_v.at[c], data_sem.at[c]),
            pltpu.make_async_copy(prof_ref.at[pl.ds(start, chunk), :], prof_v.at[c], prof_sem.at[c]),
        )

    def start_loads(order, carry):
        for copy in loads(order):
            copy.start()
        return carry

    start_loads(0, 0)
    for copy in first:
        copy.wait()
    lax.fori_loop(1, n, start_loads, 0)
    own = counts_ref[curve]
    keep = lax.broadcasted_iota(jnp.int32, (slots, 1), 0) < own
    load = load_ref[...]
    load3[...] = left3(split(load), 1)
    loadt3[...] = left3(split(load.T), 1)
    norm = jnp.sum(jnp.where(keep, load * load, 0.0), axis=0, keepdims=True)
    norms[me] = jnp.broadcast_to(norm, (NORM_ROWS, comps))
    rows_out[...] = jnp.zeros_like(rows_out)

    def compute(order, carry, after=None):
        c = chunk_at(order)
        for copy in loads(order):
            copy.wait()

        def piece(u, inner):
            start = pl.multiple_of(u * sub, sub)
            prof = prof_v[c, pl.ds(start, sub), :]
            prof2 = split(prof)
            recon = dot(load3[...], right3(prof2, 1), ((1,), (1,)))
            resid = jnp.where(keep, data_v[c, :, pl.ds(start, sub)] - recon, 0.0)
            data_v[c, :, pl.ds(start, sub)] = resid
            time = dot(loadt3[...], right3(split(resid), 0), ((1,), (0,))).T
            grad[0, c, pl.ds(start, sub), :] = time[:, :half]
            grad[1, c, pl.ds(start, sub), :] = time[:, half:]
            return inner

        if after is None:
            lax.fori_loop(0, chunk // sub, piece, 0)
        else:
            for u in range(chunk // sub):
                piece(u, 0)
                after(u)
        return carry

    def row_terms(order, carry):
        c = chunk_at(order)
        prof = prof_v[c]
        row = dot(left3(split(data_v[c]), 1), right3(split(prof), 0), ((1,), (0,)))
        square = jnp.broadcast_to(jnp.sum(prof * prof, axis=0, keepdims=True), (NORM_ROWS, comps))
        for o in range(ntm):
            rows_out[o, :span, :] += row[o * span:(o + 1) * span]
            rows_out[o, span:, :] += square
        return carry

    def row_copy(k):
        other = peers[k]
        return pltpu.make_async_remote_copy(
            src_ref=rows_out.at[other], dst_ref=rows_in.at[k],
            send_sem=row_send.at[k], recv_sem=row_recv.at[k],
            device_id={"tm": other}, device_id_type=MESH,
        )

    def new_copy(k):
        return pltpu.make_async_remote_copy(
            src_ref=rows_new.at[shard], dst_ref=rows_new.at[shard],
            send_sem=new_send.at[k], recv_sem=new_recv.at[k],
            device_id={"tm": peers[k]}, device_id_type=MESH,
        )

    def ring_copy(w, step, piece):
        sign, other = ways[w]
        c = lax.rem(me - sign * step + 2 * n, n)
        at = pl.ds(piece * part, part)
        return c, at, pltpu.make_async_remote_copy(
            src_ref=grad.at[w, c, at, :], dst_ref=came.at[w, step, at, :],
            send_sem=ring_send.at[w, step, piece], recv_sem=ring_recv.at[w, step, piece],
            device_id={"curves": other}, device_id_type=MESH,
        )

    def norm_copy(step):
        c = lax.rem(me - step + 2 * n, n)
        return pltpu.make_async_remote_copy(
            src_ref=norms.at[c], dst_ref=norms.at[c],
            send_sem=norm_send.at[step], recv_sem=norm_recv.at[step],
            device_id={"curves": ways[0][1]}, device_id_type=MESH,
        )

    def place(w, c, piece):
        rows = pl.ds(pl.multiple_of(c * chunk + piece * part, part), part)
        return new_prof_ref.at[rows, pl.ds(w * half, half)]

    def all_copy(w, step, piece):
        sign, other = ways[w]
        c = lax.rem(me + sign - sign * step + 2 * n, n)
        return pltpu.make_async_remote_copy(
            src_ref=place(w, c, piece), dst_ref=place(w, c, piece),
            send_sem=all_send.at[w, step, piece], recv_sem=all_recv.at[w, step, piece],
            device_id={"curves": other}, device_id_type=MESH,
        )

    def send_first(u):
        if u == 0:
            pl.semaphore_wait(barrier, 2 + len(peers))
        each = sub // part
        for piece in range(u * each, (u + 1) * each):
            for w in range(2):
                ring_copy(w, 0, piece)[2].start()

    compute(0, 0, send_first)
    norm_copy(0).start()

    def ring_step(step, carry):
        for w in range(2):
            lo = jnp.maximum(2 * step + w - 1, 1)
            hi = jnp.minimum(2 * step + w, n)
            lax.fori_loop(lo, hi, compute, 0)
            late = 2 * step + w - n
            lax.fori_loop(jnp.maximum(late, 0), jnp.maximum(late + 1, 0), row_terms, 0)

            for piece in range(pieces):
                c, at, copy = ring_copy(w, step, piece)

                ring_copy(w, step - 1, piece)[2].wait_recv()
                grad[w, c, at, :] = grad[w, c, at, :] + came[w, step - 1, at, :]
                copy.start()

        norm_copy(step - 1).wait_recv()
        norm_copy(step).start()
        return carry

    lax.fori_loop(1, n - 1, ring_step, 0)

    norm_copy(n - 2).wait_recv()
    total = norms[0]
    for k in range(1, n):
        total = total + norms[k]
    total = total[0:1]

    for piece in range(pieces):
        for w in range(2):
            ring_copy(w, n - 2, piece)[2].wait_recv()
            sign, _ = ways[w]
            c = lax.rem(me + sign + n, n)
            at = pl.ds(piece * part, part)
            lanes = pl.ds(w * half, half)
            summed = grad[w, c, at, :] + came[w, n - 2, at, :]
            place(w, c, piece)[...] = jnp.maximum(
                prof_v[c, at, lanes] + summed / total[:, w * half:(w + 1) * half], 0.0
            )
            all_copy(w, 0, piece).start()

    lax.fori_loop(n - 2, n, row_terms, 0)
    for k in range(ntm - 1):
        row_copy(k).start()

    def share_rows():
        for k in range(ntm - 1):
            row_copy(k).wait()
        mine = rows_out[shard]
        for k in range(ntm - 1):
            mine = mine + rows_in[k]
        base = pl.multiple_of(shard * span, span)
        alive = base + lax.broadcasted_iota(jnp.int32, (span, 1), 0) < own
        moved = load_ref[pl.ds(base, span), :] + mine[:span] / mine[span:span + 1]
        rows_new[shard] = jnp.where(alive, jnp.maximum(moved, 0.0), 0.0)
        for k in range(ntm - 1):
            new_copy(k).start()

    def all_step(step, carry):
        for piece in range(pieces):
            for w in range(2):
                all_copy(w, step - 1, piece).wait_recv()
                all_copy(w, step, piece).start()
        pl.when(step == n // 2)(share_rows)
        return carry

    lax.fori_loop(1, n - 1, all_step, 0)

    for k in range(ntm - 1):
        new_copy(k).wait()
    for o in range(ntm):
        pltpu.make_async_copy(
            rows_new.at[o], new_load_ref.at[pl.ds(o * span, span), :], rows_sem.at[o]
        ).start()

    for piece in range(pieces):
        for w in range(2):
            all_copy(w, n - 2, piece).wait_recv()

    def drain(step, carry):
        for piece in range(pieces):
            for w in range(2):
                ring_copy(w, step, piece)[2].wait_send()
                all_copy(w, step, piece).wait_send()
        norm_copy(step).wait_send()
        return carry

    lax.fori_loop(0, n - 1, drain, 0)
    for o in range(ntm):
        pltpu.make_async_copy(
            rows_new.at[o], new_load_ref.at[pl.ds(o * span, span), :], rows_sem.at[o]
        ).wait()


def local(n, ntm, curves_data, loadings, profiles, counts):
    slots, points = curves_data.shape
    comps = loadings.shape[1]
    chunk = points // n
    sub = min(chunk, 256)
    pieces = 4
    half = comps // 2
    span = slots // ntm
    f32, bf16 = jnp.float32, jnp.bfloat16
    dma = pltpu.SemaphoreType.DMA
    flops = 3 * 3 * 2 * slots * points * comps
    return pl.pallas_call(
        functools.partial(kernel, n, ntm, pieces, sub),
        out_shape=(
            pltpu.VMEM((slots, comps), f32),
            pltpu.VMEM((points, comps), f32),
        ),
        in_specs=[pl.BlockSpec(memory_space=pltpu.HBM)] * 4,
        out_specs=[pl.BlockSpec(memory_space=pltpu.VMEM)] * 2,
        scratch_shapes=[
            pltpu.SMEM((n,), jnp.int32),
            pltpu.VMEM((slots, comps), f32),
            pltpu.VMEM((n, slots, chunk), f32),
            pltpu.VMEM((n, chunk, comps), f32),
            pltpu.VMEM((slots, 3 * comps), bf16),
            pltpu.VMEM((comps, 3 * slots), bf16),
            pltpu.VMEM((2, n, chunk, half), f32),
            pltpu.VMEM((2, n - 1, chunk, half), f32),
            pltpu.VMEM((n, NORM_ROWS, comps), f32),
            pltpu.VMEM((ntm, span + NORM_ROWS, comps), f32),
            pltpu.VMEM((ntm - 1, span + NORM_ROWS, comps), f32),
            pltpu.VMEM((ntm, span, comps), f32),
            dma((n,)),
            dma((n,)),
            dma((2, n - 1, pieces)),
            dma((2, n - 1, pieces)),
            dma((2, n - 1, pieces)),
            dma((2, n - 1, pieces)),
            dma((n - 1,)),
            dma((n - 1,)),
            dma((ntm - 1,)),
            dma((ntm - 1,)),
            dma((ntm - 1,)),
            dma((ntm - 1,)),
            dma((2,)),
            dma((ntm,)),
        ],
        compiler_params=pltpu.CompilerParams(
            collective_id=0, has_side_effects=True, vmem_limit_bytes=58 * 1024 * 1024
        ),
        cost_estimate=pl.CostEstimate(
            flops=flops, bytes_accessed=4 * (slots * points + 2 * points * comps), transcendentals=0
        ),
    )(counts, curves_data, loadings, profiles)


def solution(mesh):
    return jax.shard_map(
        functools.partial(local, mesh.shape["curves"], mesh.shape["tm"]),
        mesh=mesh,
        in_specs=(P("curves", "tm"), P("curves", None), P("tm", None), P()),
        out_specs=(P("curves", None), P("tm", None)),
        check_vma=False,
    )
```

```python
import functools

import jax
import jax.numpy as jnp
from jax import lax
from jax.experimental import pallas as pl
from jax.experimental.pallas import tpu as pltpu
from jax.sharding import PartitionSpec as P

MESH = pl.DeviceIdType.MESH
NORM_ROWS = 8


def split(value):
    high = value.astype(jnp.bfloat16)
    low = (value - high.astype(jnp.float32)).astype(jnp.bfloat16)
    return high, low


def left3(pair, axis):
    return jnp.concatenate((pair[0], pair[0], pair[1]), axis=axis)


def right3(pair, axis):
    return jnp.concatenate((pair[0], pair[1], pair[0]), axis=axis)


def dot(a, b, contract):
    return lax.dot_general(a, b, (contract, ((), ())), preferred_element_type=jnp.float32)


def kernel(
    n, ntm, pieces, sub,
    counts_hbm, data_ref, load_hbm, prof_ref,
    new_load_ref, new_prof_ref,
    counts_ref, load_ref, data_v, prof_v, load3, loadt3,
    grad, came, norms, rows_out, rows_in, rows_new,
    data_sem, prof_sem, ring_send, ring_recv, all_send, all_recv, norm_send, norm_recv,
    row_send, row_recv, new_send, new_recv, first_sem, rows_sem,
):
    slots, comps = load_ref.shape
    chunk = prof_v.shape[1]
    half = comps // 2
    part = chunk // pieces
    span = slots // ntm
    curve = lax.axis_index("curves")
    shard = lax.axis_index("tm")

    line = curve // 2
    me = jnp.where(curve % 2 == 0, line, n - 1 - line)

    def device_at(place):
        place = lax.rem(place + n, n)
        return jnp.where(place < n // 2, 2 * place, 2 * (n - 1 - place) + 1)

    ways = ((1, device_at(me + 1)), (-1, device_at(me - 1)))
    peers = [lax.rem(shard + k, ntm) for k in range(1, ntm)]

    first = (
        pltpu.make_async_copy(load_hbm, load_ref, first_sem.at[0]),
        pltpu.make_async_copy(counts_hbm, counts_ref, first_sem.at[1]),
    )
    for copy in first:
        copy.start()

    barrier = pltpu.get_barrier_semaphore()
    for _, other in ways:
        pl.semaphore_signal(barrier, inc=1, device_id={"curves": other}, device_id_type=MESH)
    for other in peers:
        pl.semaphore_signal(barrier, inc=1, device_id={"tm": other}, device_id_type=MESH)

    def chunk_at(order):
        step = (order + 1) // 2
        return lax.rem(jnp.where(order % 2 == 1, me - step, me + step) + n, n)

    def loads(order):
        c = chunk_at(order)
        start = pl.multiple_of(c * chunk, chunk)
        return (
            pltpu.make_async_copy(data_ref.at[:, pl.ds(start, chunk)], data_v.at[c], data_sem.at[c]),
            pltpu.make_async_copy(prof_ref.at[pl.ds(start, chunk), :], prof_v.at[c], prof_sem.at[c]),
        )

    def start_loads(order, carry):
        for copy in loads(order):
            copy.start()
        return carry

    start_loads(0, 0)
    for copy in first:
        copy.wait()
    lax.fori_loop(1, n, start_loads, 0)
    own = counts_ref[curve]
    keep = lax.broadcasted_iota(jnp.int32, (slots, 1), 0) < own
    load = load_ref[...]
    load3[...] = left3(split(load), 1)
    loadt3[...] = left3(split(load.T), 1)
    norm = jnp.sum(jnp.where(keep, load * load, 0.0), axis=0, keepdims=True)
    norms[me] = jnp.broadcast_to(norm, (NORM_ROWS, comps))
    rows_out[...] = jnp.zeros_like(rows_out)

    def compute(order, carry):
        c = chunk_at(order)
        for copy in loads(order):
            copy.wait()

        def piece(u, inner):
            start = pl.multiple_of(u * sub, sub)
            prof = prof_v[c, pl.ds(start, sub), :]
            prof2 = split(prof)
            recon = dot(load3[...], right3(prof2, 1), ((1,), (1,)))
            resid = jnp.where(keep, data_v[c, :, pl.ds(start, sub)] - recon, 0.0)
            data_v[c, :, pl.ds(start, sub)] = resid
            time = dot(loadt3[...], right3(split(resid), 0), ((1,), (0,))).T
            grad[0, c, pl.ds(start, sub), :] = time[:, :half]
            grad[1, c, pl.ds(start, sub), :] = time[:, half:]
            return inner

        lax.fori_loop(0, chunk // sub, piece, 0)
        return carry

    def row_terms(order, carry):
        c = chunk_at(order)
        prof = prof_v[c]
        row = dot(left3(split(data_v[c]), 1), right3(split(prof), 0), ((1,), (0,)))
        square = jnp.broadcast_to(jnp.sum(prof * prof, axis=0, keepdims=True), (NORM_ROWS, comps))
        for o in range(ntm):
            rows_out[o, :span, :] += row[o * span:(o + 1) * span]
            rows_out[o, span:, :] += square
        return carry

    def row_copy(k):
        other = peers[k]
        return pltpu.make_async_remote_copy(
            src_ref=rows_out.at[other], dst_ref=rows_in.at[k],
            send_sem=row_send.at[k], recv_sem=row_recv.at[k],
            device_id={"tm": other}, device_id_type=MESH,
        )

    def new_copy(k):
        return pltpu.make_async_remote_copy(
            src_ref=rows_new.at[shard], dst_ref=rows_new.at[shard],
            send_sem=new_send.at[k], recv_sem=new_recv.at[k],
            device_id={"tm": peers[k]}, device_id_type=MESH,
        )

    def ring_copy(w, step, piece):
        sign, other = ways[w]
        c = lax.rem(me - sign * step + 2 * n, n)
        at = pl.ds(piece * part, part)
        return c, at, pltpu.make_async_remote_copy(
            src_ref=grad.at[w, c, at, :], dst_ref=came.at[w, step, at, :],
            send_sem=ring_send.at[w, step, piece], recv_sem=ring_recv.at[w, step, piece],
            device_id={"curves": other}, device_id_type=MESH,
        )

    def norm_copy(step):
        c = lax.rem(me - step + 2 * n, n)
        return pltpu.make_async_remote_copy(
            src_ref=norms.at[c], dst_ref=norms.at[c],
            send_sem=norm_send.at[step], recv_sem=norm_recv.at[step],
            device_id={"curves": ways[0][1]}, device_id_type=MESH,
        )

    def place(w, c, piece):
        rows = pl.ds(pl.multiple_of(c * chunk + piece * part, part), part)
        return new_prof_ref.at[rows, pl.ds(w * half, half)]

    def all_copy(w, step, piece):
        sign, other = ways[w]
        c = lax.rem(me + sign - sign * step + 2 * n, n)
        return pltpu.make_async_remote_copy(
            src_ref=place(w, c, piece), dst_ref=place(w, c, piece),
            send_sem=all_send.at[w, step, piece], recv_sem=all_recv.at[w, step, piece],
            device_id={"curves": other}, device_id_type=MESH,
        )

    lax.fori_loop(0, 1, compute, 0)
    pl.semaphore_wait(barrier, 2 + len(peers))

    def ring_step(step, carry):
        for w in range(2):
            lo = jnp.maximum(2 * step + w - 1, 1)
            hi = jnp.minimum(2 * step + w, n)
            lax.fori_loop(lo, hi, compute, 0)
            late = 2 * step + w - n
            lax.fori_loop(jnp.maximum(late, 0), jnp.maximum(late + 1, 0), row_terms, 0)

            for piece in range(pieces):
                c, at, copy = ring_copy(w, step, piece)

                @pl.when(step > 0)
                def _():
                    ring_copy(w, step - 1, piece)[2].wait_recv()
                    grad[w, c, at, :] = grad[w, c, at, :] + came[w, step - 1, at, :]

                copy.start()

        @pl.when(step > 0)
        def _():
            norm_copy(step - 1).wait_recv()

        norm_copy(step).start()
        return carry

    lax.fori_loop(0, n - 1, ring_step, 0)

    norm_copy(n - 2).wait_recv()
    total = norms[0]
    for k in range(1, n):
        total = total + norms[k]
    total = total[0:1]

    for piece in range(pieces):
        for w in range(2):
            ring_copy(w, n - 2, piece)[2].wait_recv()
            sign, _ = ways[w]
            c = lax.rem(me + sign + n, n)
            at = pl.ds(piece * part, part)
            lanes = pl.ds(w * half, half)
            summed = grad[w, c, at, :] + came[w, n - 2, at, :]
            place(w, c, piece)[...] = jnp.maximum(
                prof_v[c, at, lanes] + summed / total[:, w * half:(w + 1) * half], 0.0
            )
            all_copy(w, 0, piece).start()

    lax.fori_loop(n - 2, n, row_terms, 0)
    for k in range(ntm - 1):
        row_copy(k).start()

    def share_rows():
        for k in range(ntm - 1):
            row_copy(k).wait()
        mine = rows_out[shard]
        for k in range(ntm - 1):
            mine = mine + rows_in[k]
        base = pl.multiple_of(shard * span, span)
        alive = base + lax.broadcasted_iota(jnp.int32, (span, 1), 0) < own
        moved = load_ref[pl.ds(base, span), :] + mine[:span] / mine[span:span + 1]
        rows_new[shard] = jnp.where(alive, jnp.maximum(moved, 0.0), 0.0)
        for k in range(ntm - 1):
            new_copy(k).start()

    def all_step(step, carry):
        for piece in range(pieces):
            for w in range(2):
                all_copy(w, step - 1, piece).wait_recv()
                all_copy(w, step, piece).start()
        pl.when(step == n // 2)(share_rows)
        return carry

    lax.fori_loop(1, n - 1, all_step, 0)

    for k in range(ntm - 1):
        new_copy(k).wait()
    for o in range(ntm):
        pltpu.make_async_copy(
            rows_new.at[o], new_load_ref.at[pl.ds(o * span, span), :], rows_sem.at[o]
        ).start()

    for piece in range(pieces):
        for w in range(2):
            all_copy(w, n - 2, piece).wait_recv()

    def drain(step, carry):
        for piece in range(pieces):
            for w in range(2):
                ring_copy(w, step, piece)[2].wait_send()
                all_copy(w, step, piece).wait_send()
        norm_copy(step).wait_send()
        return carry

    lax.fori_loop(0, n - 1, drain, 0)
    for o in range(ntm):
        pltpu.make_async_copy(
            rows_new.at[o], new_load_ref.at[pl.ds(o * span, span), :], rows_sem.at[o]
        ).wait()


def local(n, ntm, curves_data, loadings, profiles, counts):
    slots, points = curves_data.shape
    comps = loadings.shape[1]
    chunk = points // n
    sub = min(chunk, 512)
    pieces = 2
    half = comps // 2
    span = slots // ntm
    f32, bf16 = jnp.float32, jnp.bfloat16
    dma = pltpu.SemaphoreType.DMA
    flops = 3 * 3 * 2 * slots * points * comps
    return pl.pallas_call(
        functools.partial(kernel, n, ntm, pieces, sub),
        out_shape=(
            pltpu.VMEM((slots, comps), f32),
            pltpu.VMEM((points, comps), f32),
        ),
        in_specs=[pl.BlockSpec(memory_space=pltpu.HBM)] * 4,
        out_specs=[pl.BlockSpec(memory_space=pltpu.VMEM)] * 2,
        scratch_shapes=[
            pltpu.SMEM((n,), jnp.int32),
            pltpu.VMEM((slots, comps), f32),
            pltpu.VMEM((n, slots, chunk), f32),
            pltpu.VMEM((n, chunk, comps), f32),
            pltpu.VMEM((slots, 3 * comps), bf16),
            pltpu.VMEM((comps, 3 * slots), bf16),
            pltpu.VMEM((2, n, chunk, half), f32),
            pltpu.VMEM((2, n - 1, chunk, half), f32),
            pltpu.VMEM((n, NORM_ROWS, comps), f32),
            pltpu.VMEM((ntm, span + NORM_ROWS, comps), f32),
            pltpu.VMEM((ntm - 1, span + NORM_ROWS, comps), f32),
            pltpu.VMEM((ntm, span, comps), f32),
            dma((n,)),
            dma((n,)),
            dma((2, n - 1, pieces)),
            dma((2, n - 1, pieces)),
            dma((2, n - 1, pieces)),
            dma((2, n - 1, pieces)),
            dma((n - 1,)),
            dma((n - 1,)),
            dma((ntm - 1,)),
            dma((ntm - 1,)),
            dma((ntm - 1,)),
            dma((ntm - 1,)),
            dma((2,)),
            dma((ntm,)),
        ],
        compiler_params=pltpu.CompilerParams(
            collective_id=0, has_side_effects=True, vmem_limit_bytes=58 * 1024 * 1024
        ),
        cost_estimate=pl.CostEstimate(
            flops=flops, bytes_accessed=4 * (slots * points + 2 * points * comps), transcendentals=0
        ),
    )(counts, curves_data, loadings, profiles)


def solution(mesh):
    return jax.shard_map(
        functools.partial(local, mesh.shape["curves"], mesh.shape["tm"]),
        mesh=mesh,
        in_specs=(P("curves", "tm"), P("curves", None), P("tm", None), P()),
        out_specs=(P("curves", None), P("tm", None)),
        check_vma=False,
    )
```
